512 devices in a mesh: blk: 128 (over y_lo, z, x), feat: 4 (over y_hi, core).
Axes of the slice: x: 4, y: 4 (y_hi: 2, y_lo: 2; y = y_hi * 2 + y_lo), z: 16, core: 2. Of those that a mesh axis runs over, the one named last changes fastest.
Arguments:
- image_embeds: bfloat16 [8192, 1024], P('blk', 'feat')
- text_embeds: bfloat16 [8192, 1024], P('blk', 'feat')
- logit_scale: float32 [1], replicated, may hold values from 3 to 6
Outputs:
- pair_loss: float32 [8192], P('blk')
- image_grad: float32 [8192, 1024], P('blk', 'feat')
- text_grad: float32 [8192, 1024], P('blk', 'feat')
The draws below stay inside these ranges and needn't reach their ends.
All inputs are finite; a program needn't handle non-finite values.
Results may differ from the reference program's by a relative error of at most 0.004.
Values may be sent and summed in bfloat16 or wider, within the bound.
A program may use at most 64 MiB of HBM per device.

```python
import math
import jax
import jax.numpy as jnp
from jax import lax

D = 1024
PAIRS = 8192


def shared_text(key):
    sigma = D ** (-0.5)
    normal_part = jax.random.truncated_normal(key, -6.0, 6.0, (PAIRS, D), jnp.float32) * sigma
    return normal_part


def draw_text_embeds(key, part):
    normal_part = shared_text(key)
    text = normal_part
    return text.astype(jnp.bfloat16)


def draw_image_embeds(key, part):
    key = jax.random.fold_in(key, 2)
    key_own = jax.random.fold_in(key, 0)
    image = jax.random.truncated_normal(key_own, -6.0, 6.0, (PAIRS, D), jnp.float32)
    return image.astype(jnp.bfloat16)


def setup_inputs(seed: int = 0) -> dict:
    key_list = jax.random.split(jax.random.key(seed), 4)
    image_embeds = draw_image_embeds(jax.random.fold_in(key_list[3], 71), 0)
    text_embeds = draw_text_embeds(jax.random.fold_in(key_list[3], 71), 0)
    logit_scale = jnp.clip(jnp.exp(jax.random.uniform(key_list[2], (1,), jnp.float32, math.log(3.0), math.log(6.0))), 3.0, 6.0)
    return {"image_embeds": image_embeds, "text_embeds": text_embeds, "logit_scale": logit_scale}


def reference(image_embeds, text_embeds, logit_scale):
    factor = logit_scale[0]
    block_rows = math.gcd(PAIRS, 512)
    block_count = PAIRS // block_rows

    def logits_of(first_index):
        row_block = lax.dynamic_slice_in_dim(image_embeds, first_index, block_rows, 0)
        return factor * lax.dot_general(row_block, text_embeds, (((1,), (1,)), ((), ())), preferred_element_type=jnp.float32)

    def first_pass(carry, step_index):
        col_max, col_sum = carry
        first_index = (step_index * block_rows).astype(jnp.int32)
        logits = logits_of(first_index)
        row_lse = jax.nn.logsumexp(logits, axis=1)
        own_block = lax.dynamic_slice_in_dim(logits, first_index, block_rows, 1)
        diagonal = jnp.diagonal(own_block)
        block_max = jnp.max(logits, axis=0)
        new_max = jnp.maximum(col_max, block_max)
        new_sum = col_sum * jnp.exp(col_max - new_max) + jnp.sum(jnp.exp(logits - new_max[None, :]), axis=0)
        return (new_max, new_sum), (row_lse, diagonal)

    start_max = jnp.full((PAIRS,), -1e30, jnp.float32)
    start_sum = jnp.zeros((PAIRS,), jnp.float32)
    (col_max, col_sum), (row_lse, diagonal) = lax.scan(first_pass, (start_max, start_sum), jnp.arange(block_count, dtype=jnp.int32))
    row_lse = row_lse.reshape(PAIRS)
    diagonal = diagonal.reshape(PAIRS)
    col_lse = col_max + jnp.log(col_sum)
    pair_loss = 0.5 * (row_lse + col_lse) - diagonal

    def second_pass(text_acc, step_index):
        first_index = (step_index * block_rows).astype(jnp.int32)
        logits = logits_of(first_index)
        row_part = lax.dynamic_slice_in_dim(row_lse, first_index, block_rows, 0)
        identity = (jnp.arange(PAIRS, dtype=jnp.int32)[None, :] == (first_index + jnp.arange(block_rows, dtype=jnp.int32))[:, None]).astype(jnp.float32)
        grad_logits = (0.5 * (jnp.exp(logits - row_part[:, None]) + jnp.exp(logits - col_lse[None, :])) - identity).astype(jnp.bfloat16)
        row_block = lax.dynamic_slice_in_dim(image_embeds, first_index, block_rows, 0)
        image_part = factor * jnp.dot(grad_logits, text_embeds, preferred_element_type=jnp.float32)
        text_acc = text_acc + lax.dot_general(grad_logits, row_block, (((0,), (0,)), ((), ())), preferred_element_type=jnp.float32)
        return text_acc, image_part

    text_acc, image_grad = lax.scan(second_pass, jnp.zeros((PAIRS, D), jnp.float32), jnp.arange(block_count, dtype=jnp.int32))
    return pair_loss, image_grad.reshape(PAIRS, D), factor * text_acc
```

```python
import functools

import jax
import jax.numpy as jnp
from jax import lax
from jax.experimental import pallas as pl
from jax.experimental.pallas import tpu as pltpu
from jax.sharding import PartitionSpec as P

MESH = pl.DeviceIdType.MESH
F32 = jnp.float32
BF16 = jnp.bfloat16

NX, NY, NZ = 4, 4, 16
ROWS, FEATS = 64, 256
HALF = ROWS // 2
IMG = 16 * ROWS
TXT = 8 * HALF
LANES = 128

PLANE = [(dx, dy) for dx in range(NX) for dy in range(NY) if dx or dy]
COLUMN = [(dh, dk) for dk in (4, 3, 5, 2, 6, 1, 7, 0) for dh in range(2) if dh or dk]


def where_am_i():
    blk, feat = lax.axis_index("blk"), lax.axis_index("feat")
    x = blk % NX
    z = (blk // NX) % NZ
    yl = blk // (NX * NZ)
    yh = feat // 2
    return x, yl, yh, z, feat % 2


def device(x, yl, yh, z, c):
    return {"blk": (yl * NZ + z) * NX + x, "feat": yh * 2 + c}


def kernel(
    scale_ref, img_ref, txt_ref, loss_ref, ig_ref, tg_ref,
    img_all, txt_all, logits, e_row, e_col, grad, i_part, t_part, i_recv, t_recv,
    row_own, row_max, row_recv, row_lse, row_mul, col_own, col_recv, loss_all, pair_out, pair_in,
    s_txt, r_txt, s_img, r_img, s_pair, r_pair, s_sib, r_sib,
    s_row, r_row, s_col, r_col, s_loss, r_loss, s_tp, r_tp, s_ip, r_ip, s_fin, r_fin,
):
    x, yl, yh, z, c = where_am_i()
    q, k = z % 2, z // 2
    feat = yh * 2 + c
    factor = scale_ref[0]

    def in_plane(dx, dy, dq=0):
        x2 = (x + dx) % NX
        y2 = (yh * 2 + yl + dy) % NY
        return x2, y2 % 2, y2 // 2, (z + dq) - 2 * dq * q

    def in_column(dh, dk):
        return x, yl, (yh + dh) % 2, ((k + dk) % 8) * 2 + q

    def to(place):
        return device(*place, c)

    pair = to((x, yl, yh, z + 1 - 2 * q))
    sibling = device(x, yl, yh, z, 1 - c)

    barrier = pltpu.get_barrier_semaphore()
    partners = [to(in_column(dh, dk)) for dh, dk in COLUMN]
    partners += [pair]
    partners += [to(in_plane(dx, dy, dq)) for dq in range(2) for dx, dy in PLANE if dq or (dx, dy) != (0, 2)]
    partners += [sibling]
    for partner in partners:
        pl.semaphore_signal(barrier, inc=1, device_id=partner, device_id_type=MESH)

    def image_rows(q0, p0):
        return pl.ds(pl.multiple_of((q0 * 8 + p0) * ROWS, ROWS), ROWS)

    p = yl * NX + x
    own_rows = image_rows(q, p)
    own_cols = pl.ds(pl.multiple_of(k * HALF, HALF), HALF)
    own_half = pl.ds(pl.multiple_of(yh * HALF, HALF), HALF)
    img_all[feat, own_rows, :] = img_ref[...]
    txt_all[feat, own_cols, :] = txt_ref[own_half, :]
    col_own[...] = jnp.zeros_like(col_own)
    pl.semaphore_wait(barrier, len(partners))

    started = []

    def send(src, dst, s, r, target):
        copy = pltpu.make_async_remote_copy(
            src_ref=src, dst_ref=dst, send_sem=s, recv_sem=r, device_id=target, device_id_type=MESH
        )
        copy.start()
        started.append(copy)
        return copy

    txt_copies = []
    for n, (dh, dk) in enumerate(COLUMN):
        place = in_column(dh, dk)
        half = pl.ds(pl.multiple_of(place[2] * HALF, HALF), HALF)
        txt_copies.append(
            send(txt_ref.at[half, :], txt_all.at[feat, own_cols, :], s_txt.at[n], r_txt.at[n], to(place))
        )
    own_block = img_all.at[feat, own_rows, :]
    swap = send(img_ref, own_block, s_pair, r_pair, pair)
    direct = [
        send(img_ref, own_block, s_img.at[0, n], r_img.at[0, n], to(in_plane(dx, dy)))
        for n, (dx, dy) in enumerate(PLANE)
    ]
    swap.wait_recv()
    pair_block = img_all.at[feat, image_rows(1 - q, p), :]
    passed = [
        send(pair_block, pair_block, s_img.at[1, n], r_img.at[1, n], to(in_plane(dx, dy)))
        for n, (dx, dy) in enumerate(PLANE)
    ]

    def share_image(slot, q0):
        copies = []
        for h in range(2):
            part = img_all.at[2 * h + c, pl.ds(pl.multiple_of(q0 * 8 * ROWS, 8 * ROWS), 8 * ROWS), :]
            copies.append(send(part, part, s_sib.at[slot, h], r_sib.at[slot, h], sibling))
        return copies

    shared = []
    for copy in direct:
        copy.wait_recv()
    shared += share_image(0, q)
    for copy in txt_copies:
        copy.wait_recv()
    for h in range(2):
        part = txt_all.at[2 * h + c]
        shared.append(send(part, part, s_sib.at[1, h], r_sib.at[1, h], sibling))
    for copy in passed:
        copy.wait_recv()
    shared += share_image(2, 1 - q)
    for copy in shared:
        copy.wait_recv()

    eye = lax.broadcasted_iota(jnp.int32, (LANES, LANES), 0) == lax.broadcasted_iota(jnp.int32, (LANES, LANES), 1)

    def to_lanes(column):
        return jnp.sum(jnp.where(eye, column, 0.0), axis=0, keepdims=True)

    def to_rows(lanes):
        return jnp.sum(jnp.where(eye, lanes, 0.0), axis=1, keepdims=True)

    col_max = None
    for b in range(IMG // LANES):
        rows = pl.ds(b * LANES, LANES)
        total = None
        for f in range(4):
            term = lax.dot_general(
                img_all[f, rows, :], txt_all[f], (((1,), (1,)), ((), ())), preferred_element_type=F32
            )
            total = term if total is None else total + term
        value = factor * total
        logits[rows, :] = value
        largest = jnp.max(value, axis=1, keepdims=True)
        shifted = jnp.exp(value - largest)
        e_row[rows, :] = shifted
        lse = largest + jnp.log(jnp.sum(shifted, axis=1, keepdims=True))
        row_own[pl.ds(b, 1), :] = to_lanes(lse)
        row_max[pl.ds(b, 1), :] = to_lanes(largest)
        block_max = jnp.max(value, axis=0, keepdims=True)
        col_max = block_max if col_max is None else jnp.maximum(col_max, block_max)

    row_slot = row_recv.at[q * 16 + (yh * 2 + yl) * NX + x]
    row_copies = []
    for dq in range(2):
        for n, (dx, dy) in enumerate([(0, 0)] + PLANE):
            if dq or n:
                row_copies.append(
                    send(row_own, row_slot, s_row.at[dq, n], r_row.at[dq, n], to(in_plane(dx, dy, dq)))
                )
    row_slot[...] = row_own[...]

    col_sum = jnp.zeros((1, TXT), F32)
    for b in range(IMG // LANES):
        rows = pl.ds(b * LANES, LANES)
        shifted = jnp.exp(logits[rows, :] - col_max)
        e_col[rows, :] = shifted
        col_sum = col_sum + jnp.sum(shifted, axis=0, keepdims=True)
    lse = col_max + jnp.log(col_sum)
    col_own[pl.ds(0, 1), :] = lse[:, :LANES]
    col_own[pl.ds(1, 1), :] = lse[:, LANES:]
    col_slot = col_recv.at[k]
    col_copies = [
        send(col_own, col_slot, s_col.at[dk], r_col.at[dk], to(in_column(0, dk))) for dk in (4, 3, 5, 2, 6, 1, 7)
    ]
    col_slot[...] = col_own[...]

    for copy in row_copies:
        copy.wait_recv()
    for copy in col_copies:
        copy.wait_recv()

    def combine(parts):
        largest = jnp.max(parts, axis=0)
        return largest + jnp.log(jnp.sum(jnp.exp(parts - largest[None]), axis=0))

    row_total = combine(row_recv[...])
    row_lse[...] = row_total
    row_mul[...] = 0.5 * jnp.exp(row_max[...] - row_total)
    col_total = combine(col_recv[...])
    col_lse = jnp.concatenate([col_total[0:1], col_total[1:2]], axis=1)
    col_mul = 0.5 * jnp.exp(col_max - col_lse)

    for b in range(IMG // LANES):
        rows = pl.ds(b * LANES, LANES)
        row_factor = to_rows(row_mul[pl.ds(b, 1), :])
        grad[rows, :] = (e_row[rows, :] * row_factor + e_col[rows, :] * col_mul).astype(BF16)
    first = (q * 8 + p) * ROWS + yh * HALF
    diag_rows = pl.ds(pl.multiple_of(first, HALF), HALF)
    row_id = lax.broadcasted_iota(jnp.int32, (HALF, LANES), 0)
    lane_id = lax.broadcasted_iota(jnp.int32, (HALF, LANES), 1)
    pick = lane_id - first % LANES == row_id
    line = pl.ds(first // LANES, 1)
    diag_mul = jnp.sum(jnp.where(pick, row_mul[line, :], 0.0), axis=1, keepdims=True)
    diag_lse = jnp.sum(jnp.where(pick, row_lse[line, :], 0.0), axis=1, keepdims=True)
    row_id = lax.broadcasted_iota(jnp.int32, (HALF, TXT), 0)
    lane_id = lax.broadcasted_iota(jnp.int32, (HALF, TXT), 1)
    unit = lane_id - k * HALF == row_id
    grad[diag_rows, :] = (
        e_row[diag_rows, :] * diag_mul + e_col[diag_rows, :] * col_mul - unit.astype(F32)
    ).astype(BF16)
    loss = jnp.sum(
        jnp.where(unit, 0.5 * (diag_lse + col_lse) - logits[diag_rows, :], 0.0), axis=1, keepdims=True
    )
    loss_all[own_half, :] = jnp.broadcast_to(loss, (HALF, LANES))
    loss_part = loss_all.at[own_half, :]
    loss_copy = send(loss_part, loss_part, s_loss, r_loss, to(in_column(1, 0)))

    for h in range(2):
        t_part[h] = lax.dot_general(
            grad[...], img_all[2 * h + c], (((0,), (0,)), ((), ())), preferred_element_type=F32
        ).astype(BF16)
    tp_copies = []
    for n, (dh, dk) in enumerate(COLUMN):
        place = in_column(dh, dk)
        rows = pl.ds(pl.multiple_of(((k + dk) % 8) * HALF, HALF), HALF)
        tp_copies.append(
            send(t_part.at[place[2], rows, :], t_recv.at[yh, k], s_tp.at[n], r_tp.at[n], to(place))
        )
    t_recv[yh, k] = t_part[yh, own_cols, :]

    ip_copies = []
    for turn in range(2):
        q2 = 1 - q if turn == 0 else q
        rows = pl.ds(pl.multiple_of(q2 * 8 * ROWS, 8 * ROWS), 8 * ROWS)
        for h in range(2):
            i_part[h, rows, :] = jnp.dot(
                grad[rows, :], txt_all[2 * h + c], preferred_element_type=F32
            ).astype(BF16)
        slot = (yh * 2 + yl) * NX + x
        copies = []
        for n, (dx, dy) in enumerate(PLANE):
            place = in_plane(dx, dy)
            block = i_part.at[place[2], image_rows(q2, place[1] * NX + place[0]), :]
            copies.append(send(block, i_recv.at[turn, slot], s_ip.at[turn, n], r_ip.at[turn, n], to(place)))
        i_recv[turn, slot] = i_part[yh, image_rows(q2, p), :]
        ip_copies.append(copies)

    def total_of(ref, count):
        value = ref[0].astype(F32)
        for n in range(1, count):
            value = value + ref[n].astype(F32)
        return value

    for copy in ip_copies[0]:
        copy.wait_recv()
    pair_out[...] = total_of(i_recv.at[0], 16)
    final = send(pair_out, pair_in, s_fin, r_fin, pair)
    for copy in tp_copies:
        copy.wait_recv()
    for h in range(2):
        tg_ref[pl.ds(h * HALF, HALF), :] = total_of(t_recv.at[h], 8)
    loss_copy.wait_recv()
    square = lax.broadcasted_iota(jnp.int32, (ROWS, LANES), 0) == lax.broadcasted_iota(jnp.int32, (ROWS, LANES), 1)
    loss_ref[...] = jnp.sum(jnp.where(square, loss_all[...], 0.0), axis=0, keepdims=True)[:, :ROWS]
    for copy in ip_copies[1]:
        copy.wait_recv()
    own = total_of(i_recv.at[1], 16)
    final.wait_recv()
    ig_ref[...] = own + pair_in[...]
    for copy in started:
        copy.wait_send()


def per_device(image_embeds, text_embeds, logit_scale):
    vmem = pl.BlockSpec(memory_space=pltpu.VMEM)
    dma = pltpu.SemaphoreType.DMA
    column, plane = len(COLUMN), len(PLANE)
    loss, image_grad, text_grad = pl.pallas_call(
        kernel,
        out_shape=(
            jax.ShapeDtypeStruct((1, ROWS), F32),
            jax.ShapeDtypeStruct((ROWS, FEATS), F32),
            jax.ShapeDtypeStruct((ROWS, FEATS), F32),
        ),
        in_specs=[pl.BlockSpec(memory_space=pltpu.SMEM), vmem, vmem],
        out_specs=(vmem, vmem, vmem),
        scratch_shapes=[
            pltpu.VMEM((4, IMG, FEATS), BF16),
            pltpu.VMEM((4, TXT, FEATS), BF16),
            pltpu.VMEM((IMG, TXT), F32),
            pltpu.VMEM((IMG, TXT), F32),
            pltpu.VMEM((IMG, TXT), F32),
            pltpu.VMEM((IMG, TXT), BF16),
            pltpu.VMEM((2, IMG, FEATS), BF16),
            pltpu.VMEM((2, TXT, FEATS), BF16),
            pltpu.VMEM((2, 16, ROWS, FEATS), BF16),
            pltpu.VMEM((2, 8, HALF, FEATS), BF16),
            pltpu.VMEM((8, LANES), F32),
            pltpu.VMEM((8, LANES), F32),
            pltpu.VMEM((32, 8, LANES), F32),
            pltpu.VMEM((8, LANES), F32),
            pltpu.VMEM((8, LANES), F32),
            pltpu.VMEM((8, LANES), F32),
            pltpu.VMEM((8, 8, LANES), F32),
            pltpu.VMEM((ROWS, LANES), F32),
            pltpu.VMEM((ROWS, FEATS), F32),
            pltpu.VMEM((ROWS, FEATS), F32),
            dma((column,)), dma((column,)),
            dma((2, plane)), dma((2, plane)),
            dma, dma,
            dma((3, 2)), dma((3, 2)),
            dma((2, 16)), dma((2, 16)),
            dma((8,)), dma((8,)),
            dma, dma,
            dma((column,)), dma((column,)),
            dma((2, plane)), dma((2, plane)),
            dma, dma,
        ],
        compiler_params=pltpu.CompilerParams(
            collective_id=0, has_side_effects=True, vmem_limit_bytes=48 << 20
        ),
    )(logit_scale, image_embeds, text_embeds)
    factor = logit_scale[0]
    return loss.reshape(ROWS), factor * image_grad, factor * text_grad


def solution(mesh):
    return jax.shard_map(
        per_device,
        mesh=mesh,
        in_specs=(P("blk", "feat"), P("blk", "feat"), P()),
        out_specs=(P("blk"), P("blk", "feat"), P("blk", "feat")),
        check_vma=False,
    )
```

```python
import functools

import jax
import jax.numpy as jnp
from jax import lax
from jax.experimental import pallas as pl
from jax.experimental.pallas import tpu as pltpu
from jax.sharding import PartitionSpec as P

MESH = pl.DeviceIdType.MESH
F32 = jnp.float32
BF16 = jnp.bfloat16

NX, NY, NZ = 4, 4, 16
ROWS, FEATS = 64, 256
HALF = ROWS // 2
IMG = 16 * ROWS
TXT = 8 * HALF
LANES = 128

PLANE = [(dx, dy) for dx in range(NX) for dy in range(NY) if dx or dy]
FAR = (4, 3, 5, 2, 6, 1, 7)
COLUMN = [(dh, dk) for dk in FAR for dh in range(2)] + [(1, 0)]


def where_am_i():
    blk, feat = lax.axis_index("blk"), lax.axis_index("feat")
    x = blk % NX
    z = (blk // NX) % NZ
    yl = blk // (NX * NZ)
    yh = feat // 2
    return x, yl, yh, z, feat % 2


def device(x, yl, yh, z, c):
    return {"blk": (yl * NZ + z) * NX + x, "feat": yh * 2 + c}


def kernel(
    scale_ref, img_hbm, txt_hbm, loss_ref, ig_ref, tg_ref,
    txt_own,
    img_all, txt_all, logits, e_row, e_col, grad, i_part, t_part, i_recv, t_recv,
    row_own, row_max, row_recv, row_lse, row_mul, col_own, col_recv, loss_all, pair_out, pair_in,
    s_txt, r_txt, s_img, r_img, s_pair, r_pair, s_sib, r_sib, s_sibt, r_sibt, s_sibp, r_sibp,
    s_row, r_row, s_col, r_col, s_loss, r_loss, s_tp, r_tp, s_ip, r_ip, s_fin, r_fin, s_load,
):
    x, yl, yh, z, c = where_am_i()
    q, k = z % 2, z // 2
    feat = yh * 2 + c
    factor = scale_ref[0]

    def in_plane(dx, dy, dq=0):
        x2 = (x + dx) % NX
        y2 = (yh * 2 + yl + dy) % NY
        return x2, y2 % 2, y2 // 2, (z + dq) - 2 * dq * q

    def in_column(dh, dk):
        return x, yl, (yh + dh) % 2, ((k + dk) % 8) * 2 + q

    def to(place):
        return device(*place, c)

    pair = to((x, yl, yh, z + 1 - 2 * q))
    sibling = device(x, yl, yh, z, 1 - c)

    barrier = pltpu.get_barrier_semaphore()
    partners = [to(in_column(0, dk)) for dk in FAR]
    partners += [to(in_plane(dx, dy)) for dx, dy in PLANE]
    partners += [pair, sibling]
    for partner in partners:
        pl.semaphore_signal(barrier, inc=1, device_id=partner, device_id_type=MESH)

    def image_rows(q0, p0):
        return pl.ds(pl.multiple_of((q0 * 8 + p0) * ROWS, ROWS), ROWS)

    p = yl * NX + x
    own_rows = image_rows(q, p)
    own_cols = pl.ds(pl.multiple_of(k * HALF, HALF), HALF)
    own_half = pl.ds(pl.multiple_of(yh * HALF, HALF), HALF)
    own_block = img_all.at[feat, own_rows, :]
    loads = [
        pltpu.make_async_copy(img_hbm, own_block, s_load.at[0]),
        pltpu.make_async_copy(txt_hbm, txt_own, s_load.at[1]),
    ]
    for load in loads:
        load.start()
    col_own[...] = jnp.zeros_like(col_own)
    for load in loads:
        load.wait()
    txt_all[feat, own_cols, :] = txt_own[own_half, :]
    pl.semaphore_wait(barrier, len(partners))

    started = []

    def send(src, dst, s, r, target):
        copy = pltpu.make_async_remote_copy(
            src_ref=src, dst_ref=dst, send_sem=s, recv_sem=r, device_id=target, device_id_type=MESH
        )
        copy.start()
        started.append(copy)
        return copy

    swap = send(own_block, own_block, s_pair, r_pair, pair)
    other_half = pl.ds(pl.multiple_of((1 - yh) * HALF, HALF), HALF)
    own_text = txt_all.at[feat, own_cols, :]
    cross = send(txt_own.at[other_half, :], own_text, s_txt.at[1, 0], r_txt.at[1, 0], to(in_column(1, 0)))
    txt_copies = {
        (0, dk): send(own_text, own_text, s_txt.at[0, dk], r_txt.at[0, dk], to(in_column(0, dk))) for dk in FAR
    }
    direct = [
        send(own_block, own_block, s_img.at[0, n], r_img.at[0, n], to(in_plane(dx, dy)))
        for n, (dx, dy) in enumerate(PLANE)
    ]
    cross.wait_recv()
    cross_text = txt_all.at[2 * (1 - yh) + c, own_cols, :]
    for dk in FAR:
        txt_copies[1, dk] = send(cross_text, cross_text, s_txt.at[1, dk], r_txt.at[1, dk], to(in_column(0, dk)))
    swap.wait_recv()
    pair_block = img_all.at[feat, image_rows(1 - q, p), :]
    passed = [
        send(pair_block, pair_block, s_img.at[1, n], r_img.at[1, n], to(in_plane(dx, dy)))
        for n, (dx, dy) in enumerate(PLANE)
    ]

    shared = []
    for copy in direct:
        copy.wait_recv()
    for h in range(2):
        part = img_all.at[2 * h + c, pl.ds(pl.multiple_of(q * 8 * ROWS, 8 * ROWS), 8 * ROWS), :]
        shared.append(send(part, part, s_sib.at[h], r_sib.at[h], sibling))
    shared.append(send(pair_block, pair_block, s_sibp.at[0], r_sibp.at[0], sibling))
    for dk in (0,) + FAR[::-1]:
        for dh in range(2):
            if dk:
                txt_copies[dh, dk].wait_recv()
            rows = pl.ds(pl.multiple_of(((k - dk + 8) % 8) * HALF, HALF), HALF)
            part = txt_all.at[2 * ((yh + dh) % 2) + c, rows, :]
            shared.append(send(part, part, s_sibt.at[dh, dk], r_sibt.at[dh, dk], sibling))
    for n, (dx, dy) in enumerate(PLANE):
        passed[n].wait_recv()
        x2, yl2, yh2, _ = in_plane(-dx, -dy)
        part = img_all.at[2 * yh2 + c, image_rows(1 - q, yl2 * NX + x2), :]
        shared.append(send(part, part, s_sibp.at[n + 1], r_sibp.at[n + 1], sibling))
    for copy in shared:
        copy.wait_recv()

    eye = lax.broadcasted_iota(jnp.int32, (LANES, LANES), 0) == lax.broadcasted_iota(jnp.int32, (LANES, LANES), 1)

    def to_lanes(column):
        return jnp.sum(jnp.where(eye, column, 0.0), axis=0, keepdims=True)

    def to_rows(lanes):
        return jnp.sum(jnp.where(eye, lanes, 0.0), axis=1, keepdims=True)

    col_max = None
    for b in range(IMG // LANES):
        rows = pl.ds(b * LANES, LANES)
        total = None
        for f in range(4):
            term = lax.dot_general(
                img_all[f, rows, :], txt_all[f], (((1,), (1,)), ((), ())), preferred_element_type=F32
            )
            total = term if total is None else total + term
        value = factor * total
        logits[rows, :] = value
        largest = jnp.max(value, axis=1, keepdims=True)
        shifted = jnp.exp(value - largest)
        e_row[rows, :] = shifted
        lse = largest + jnp.log(jnp.sum(shifted, axis=1, keepdims=True))
        row_own[pl.ds(b, 1), :] = to_lanes(lse)
        row_max[pl.ds(b, 1), :] = to_lanes(largest)
        block_max = jnp.max(value, axis=0, keepdims=True)
        col_max = block_max if col_max is None else jnp.maximum(col_max, block_max)

    row_slot = row_recv.at[q * 16 + (yh * 2 + yl) * NX + x]
    row_copies = []
    for dq in range(2):
        for n, (dx, dy) in enumerate([(0, 0)] + PLANE):
            if dq or n:
                row_copies.append(
                    send(row_own, row_slot, s_row.at[dq, n], r_row.at[dq, n], to(in_plane(dx, dy, dq)))
                )
    row_slot[...] = row_own[...]

    col_sum = jnp.zeros((1, TXT), F32)
    for b in range(IMG // LANES):
        rows = pl.ds(b * LANES, LANES)
        shifted = jnp.exp(logits[rows, :] - col_max)
        e_col[rows, :] = shifted
        col_sum = col_sum + jnp.sum(shifted, axis=0, keepdims=True)
    lse = col_max + jnp.log(col_sum)
    col_own[pl.ds(0, 1), :] = lse[:, :LANES]
    col_own[pl.ds(1, 1), :] = lse[:, LANES:]
    col_slot = col_recv.at[k]
    col_copies = [
        send(col_own, col_slot, s_col.at[dk], r_col.at[dk], to(in_column(0, dk))) for dk in FAR
    ]
    col_slot[...] = col_own[...]

    for copy in row_copies:
        copy.wait_recv()
    for copy in col_copies:
        copy.wait_recv()

    def combine(parts):
        largest = jnp.max(parts, axis=0)
        return largest + jnp.log(jnp.sum(jnp.exp(parts - largest[None]), axis=0))

    row_total = combine(row_recv[...])
    row_lse[...] = row_total
    row_mul[...] = 0.5 * jnp.exp(row_max[...] - row_total)
    col_total = combine(col_recv[...])
    col_lse = jnp.concatenate([col_total[0:1], col_total[1:2]], axis=1)
    col_mul = 0.5 * jnp.exp(col_max - col_lse)

    for b in range(IMG // LANES):
        rows = pl.ds(b * LANES, LANES)
        row_factor = to_rows(row_mul[pl.ds(b, 1), :])
        grad[rows, :] = (e_row[rows, :] * row_factor + e_col[rows, :] * col_mul).astype(BF16)
    first = (q * 8 + p) * ROWS + yh * HALF
    diag_rows = pl.ds(pl.multiple_of(first, HALF), HALF)
    row_id = lax.broadcasted_iota(jnp.int32, (HALF, LANES), 0)
    lane_id = lax.broadcasted_iota(jnp.int32, (HALF, LANES), 1)
    pick = lane_id - first % LANES == row_id
    line = pl.ds(first // LANES, 1)
    diag_mul = jnp.sum(jnp.where(pick, row_mul[line, :], 0.0), axis=1, keepdims=True)
    diag_lse = jnp.sum(jnp.where(pick, row_lse[line, :], 0.0), axis=1, keepdims=True)
    row_id = lax.broadcasted_iota(jnp.int32, (HALF, TXT), 0)
    lane_id = lax.broadcasted_iota(jnp.int32, (HALF, TXT), 1)
    unit = lane_id - k * HALF == row_id
    grad[diag_rows, :] = (
        e_row[diag_rows, :] * diag_mul + e_col[diag_rows, :] * col_mul - unit.astype(F32)
    ).astype(BF16)
    loss = jnp.sum(
        jnp.where(unit, 0.5 * (diag_lse + col_lse) - logits[diag_rows, :], 0.0), axis=1, keepdims=True
    )
    loss_all[own_half, :] = jnp.broadcast_to(loss, (HALF, LANES))
    loss_part = loss_all.at[own_half, :]
    loss_copy = send(loss_part, loss_part, s_loss, r_loss, to(in_column(1, 0)))

    for h in range(2):
        t_part[h] = lax.dot_general(
            grad[...], img_all[2 * h + c], (((0,), (0,)), ((), ())), preferred_element_type=F32
        ).astype(BF16)
    tp_copies = []
    for n, (dh, dk) in enumerate(COLUMN):
        place = in_column(dh, dk)
        rows = pl.ds(pl.multiple_of(((k + dk) % 8) * HALF, HALF), HALF)
        tp_copies.append(
            send(t_part.at[place[2], rows, :], t_recv.at[yh, k], s_tp.at[n], r_tp.at[n], to(place))
        )
    t_recv[yh, k] = t_part[yh, own_cols, :]

    ip_copies = []
    for turn in range(2):
        q2 = 1 - q if turn == 0 else q
        rows = pl.ds(pl.multiple_of(q2 * 8 * ROWS, 8 * ROWS), 8 * ROWS)
        for h in range(2):
            i_part[h, rows, :] = jnp.dot(
                grad[rows, :], txt_all[2 * h + c], preferred_element_type=F32
            ).astype(BF16)
        slot = (yh * 2 + yl) * NX + x
        copies = []
        for n, (dx, dy) in enumerate(PLANE):
            place = in_plane(dx, dy)
            block = i_part.at[place[2], image_rows(q2, place[1] * NX + place[0]), :]
            copies.append(send(block, i_recv.at[turn, slot], s_ip.at[turn, n], r_ip.at[turn, n], to(place)))
        i_recv[turn, slot] = i_part[yh, image_rows(q2, p), :]
        ip_copies.append(copies)

    def total_of(ref, count):
        value = ref[0].astype(F32)
        for n in range(1, count):
            value = value + ref[n].astype(F32)
        return value

    for copy in ip_copies[0]:
        copy.wait_recv()
    pair_out[...] = total_of(i_recv.at[0], 16)
    final = send(pair_out, pair_in, s_fin, r_fin, pair)
    for copy in tp_copies:
        copy.wait_recv()
    for h in range(2):
        tg_ref[pl.ds(h * HALF, HALF), :] = total_of(t_recv.at[h], 8)
    loss_copy.wait_recv()
    square = lax.broadcasted_iota(jnp.int32, (ROWS, LANES), 0) == lax.broadcasted_iota(jnp.int32, (ROWS, LANES), 1)
    loss_ref[...] = jnp.sum(jnp.where(square, loss_all[...], 0.0), axis=0, keepdims=True)[:, :ROWS]
    for copy in ip_copies[1]:
        copy.wait_recv()
    own = total_of(i_recv.at[1], 16)
    final.wait_recv()
    ig_ref[...] = own + pair_in[...]
    for copy in started:
        copy.wait_send()


def per_device(image_embeds, text_embeds, logit_scale):
    vmem = pl.BlockSpec(memory_space=pltpu.VMEM)
    hbm = pl.BlockSpec(memory_space=pltpu.HBM)
    dma = pltpu.SemaphoreType.DMA
    column, plane = len(COLUMN), len(PLANE)
    loss, image_grad, text_grad = pl.pallas_call(
        kernel,
        out_shape=(
            jax.ShapeDtypeStruct((1, ROWS), F32),
            jax.ShapeDtypeStruct((ROWS, FEATS), F32),
            jax.ShapeDtypeStruct((ROWS, FEATS), F32),
        ),
        in_specs=[pl.BlockSpec(memory_space=pltpu.SMEM), hbm, hbm],
        out_specs=(vmem, vmem, vmem),
        scratch_shapes=[
            pltpu.VMEM((ROWS, FEATS), BF16),
            pltpu.VMEM((4, IMG, FEATS), BF16),
            pltpu.VMEM((4, TXT, FEATS), BF16),
            pltpu.VMEM((IMG, TXT), F32),
            pltpu.VMEM((IMG, TXT), F32),
            pltpu.VMEM((IMG, TXT), F32),
            pltpu.VMEM((IMG, TXT), BF16),
            pltpu.VMEM((2, IMG, FEATS), BF16),
            pltpu.VMEM((2, TXT, FEATS), BF16),
            pltpu.VMEM((2, 16, ROWS, FEATS), BF16),
            pltpu.VMEM((2, 8, HALF, FEATS), BF16),
            pltpu.VMEM((8, LANES), F32),
            pltpu.VMEM((8, LANES), F32),
            pltpu.VMEM((32, 8, LANES), F32),
            pltpu.VMEM((8, LANES), F32),
            pltpu.VMEM((8, LANES), F32),
            pltpu.VMEM((8, LANES), F32),
            pltpu.VMEM((8, 8, LANES), F32),
            pltpu.VMEM((ROWS, LANES), F32),
            pltpu.VMEM((ROWS, FEATS), F32),
            pltpu.VMEM((ROWS, FEATS), F32),
            dma((2, 8)), dma((2, 8)),
            dma((2, plane)), dma((2, plane)),
            dma, dma,
            dma((2,)), dma((2,)),
            dma((2, 8)), dma((2, 8)),
            dma((16,)), dma((16,)),
            dma((2, 16)), dma((2, 16)),
            dma((8,)), dma((8,)),
            dma, dma,
            dma((column,)), dma((column,)),
            dma((2, plane)), dma((2, plane)),
            dma, dma,
            dma((2,)),
        ],
        compiler_params=pltpu.CompilerParams(
            collective_id=0, has_side_effects=True, vmem_limit_bytes=48 << 20
        ),
    )(logit_scale, image_embeds, text_embeds)
    factor = logit_scale[0]
    return loss.reshape(ROWS), factor * image_grad, factor * text_grad


def solution(mesh):
    return jax.shard_map(
        per_device,
        mesh=mesh,
        in_specs=(P("blk", "feat"), P("blk", "feat"), P()),
        out_specs=(P("blk"), P("blk", "feat"), P("blk", "feat")),
        check_vma=False,
    )
```

```python
import functools

import jax
import jax.numpy as jnp
from jax import lax
from jax.experimental import pallas as pl
from jax.experimental.pallas import tpu as pltpu
from jax.sharding import PartitionSpec as P

MESH = pl.DeviceIdType.MESH
F32 = jnp.float32
BF16 = jnp.bfloat16

NX, NY, NZ = 4, 4, 16
ROWS, FEATS = 64, 256
HALF = ROWS // 2
IMG = 16 * ROWS
TXT = 8 * HALF
LANES = 128

PLANE = sorted([(dx, dy) for dx in range(NX) for dy in range(NY) if dx or dy], key=lambda o: min(o[0], 4 - o[0]) + min(o[1], 4 - o[1]))
FAR = (4, 3, 5, 2, 6, 1, 7)
COLUMN = [(dh, dk) for dk in FAR for dh in range(2)] + [(1, 0)]


def where_am_i():
    blk, feat = lax.axis_index("blk"), lax.axis_index("feat")
    x = blk % NX
    z = (blk // NX) % NZ
    yl = blk // (NX * NZ)
    yh = feat // 2
    return x, yl, yh, z, feat % 2


def device(x, yl, yh, z, c):
    return {"blk": (yl * NZ + z) * NX + x, "feat": yh * 2 + c}


def kernel(
    scale_ref, img_hbm, txt_hbm, loss_ref, ig_ref, tg_ref,
    txt_own,
    img_all, txt_all, logits, e_row, e_col, grad, i_part, t_part, i_recv, t_recv,
    row_own, row_max, row_recv, row_lse, row_mul, col_own, col_recv, loss_all, pair_out, pair_in,
    s_txt, r_txt, s_img, r_img, s_pair, r_pair, s_sib, r_sib, s_sibt, r_sibt, s_sibp, r_sibp,
    s_row, r_row, s_col, r_col, s_loss, r_loss, s_tp, r_tp, s_ip, r_ip, s_fin, r_fin, s_load,
):
    x, yl, yh, z, c = where_am_i()
    q, k = z % 2, z // 2
    feat = yh * 2 + c
    factor = scale_ref[0]

    def in_plane(dx, dy, dq=0):
        x2 = (x + dx) % NX
        y2 = (yh * 2 + yl + dy) % NY
        return x2, y2 % 2, y2 // 2, (z + dq) - 2 * dq * q

    def in_column(dh, dk):
        return x, yl, (yh + dh) % 2, ((k + dk) % 8) * 2 + q

    def to(place):
        return device(*place, c)

    pair = to((x, yl, yh, z + 1 - 2 * q))
    sibling = device(x, yl, yh, z, 1 - c)

    barrier = pltpu.get_barrier_semaphore()
    partners = [to(in_column(0, dk)) for dk in FAR]
    partners += [to(in_plane(dx, dy)) for dx, dy in PLANE]
    partners += [pair, sibling]
    for partner in partners:
        pl.semaphore_signal(barrier, inc=1, device_id=partner, device_id_type=MESH)

    def image_rows(q0, p0):
        return pl.ds(pl.multiple_of((q0 * 8 + p0) * ROWS, ROWS), ROWS)

    p = yl * NX + x
    own_rows = image_rows(q, p)
    own_cols = pl.ds(pl.multiple_of(k * HALF, HALF), HALF)
    own_half = pl.ds(pl.multiple_of(yh * HALF, HALF), HALF)
    own_block = img_all.at[feat, own_rows, :]
    loads = [
        pltpu.make_async_copy(img_hbm, own_block, s_load.at[0]),
        pltpu.make_async_copy(txt_hbm, txt_own, s_load.at[1]),
    ]
    for load in loads:
        load.start()
    col_own[...] = jnp.zeros_like(col_own)
    for load in loads:
        load.wait()
    txt_all[feat, own_cols, :] = txt_own[own_half, :]
    pl.semaphore_wait(barrier, len(partners))

    started = []

    def send(src, dst, s, r, target):
        copy = pltpu.make_async_remote_copy(
            src_ref=src, dst_ref=dst, send_sem=s, recv_sem=r, device_id=target, device_id_type=MESH
        )
        copy.start()
        started.append(copy)
        return copy

    swap = send(own_block, own_block, s_pair, r_pair, pair)
    other_half = pl.ds(pl.multiple_of((1 - yh) * HALF, HALF), HALF)
    own_text = txt_all.at[feat, own_cols, :]
    cross = send(txt_own.at[other_half, :], own_text, s_txt.at[1, 0], r_txt.at[1, 0], to(in_column(1, 0)))
    txt_copies = {
        (0, dk): send(own_text, own_text, s_txt.at[0, dk], r_txt.at[0, dk], to(in_column(0, dk))) for dk in FAR
    }
    direct = [
        send(own_block, own_block, s_img.at[0, n], r_img.at[0, n], to(in_plane(dx, dy)))
        for n, (dx, dy) in enumerate(PLANE)
    ]
    swap.wait_recv()
    pair_block = img_all.at[feat, image_rows(1 - q, p), :]
    passed = [
        send(pair_block, pair_block, s_img.at[1, n], r_img.at[1, n], to(in_plane(dx, dy)))
        for n, (dx, dy) in enumerate(PLANE)
    ]

    cross.wait_recv()
    cross_text = txt_all.at[2 * (1 - yh) + c, own_cols, :]
    for dk in FAR:
        txt_copies[1, dk] = send(cross_text, cross_text, s_txt.at[1, dk], r_txt.at[1, dk], to(in_column(0, dk)))
    shared = []
    for copy in direct:
        copy.wait_recv()
    for h in range(2):
        part = img_all.at[2 * h + c, pl.ds(pl.multiple_of(q * 8 * ROWS, 8 * ROWS), 8 * ROWS), :]
        shared.append(send(part, part, s_sib.at[h], r_sib.at[h], sibling))
    shared.append(send(pair_block, pair_block, s_sibp.at[0], r_sibp.at[0], sibling))
    for dk in (0,) + FAR[::-1]:
        for dh in range(2):
            if dk:
                txt_copies[dh, dk].wait_recv()
            rows = pl.ds(pl.multiple_of(((k - dk + 8) % 8) * HALF, HALF), HALF)
            part = txt_all.at[2 * ((yh + dh) % 2) + c, rows, :]
            shared.append(send(part, part, s_sibt.at[dh, dk], r_sibt.at[dh, dk], sibling))
    for n, (dx, dy) in enumerate(PLANE):
        passed[n].wait_recv()
        x2, yl2, yh2, _ = in_plane(-dx, -dy)
        part = img_all.at[2 * yh2 + c, image_rows(1 - q, yl2 * NX + x2), :]
        shared.append(send(part, part, s_sibp.at[n + 1], r_sibp.at[n + 1], sibling))
    for copy in shared:
        copy.wait_recv()

    eye = lax.broadcasted_iota(jnp.int32, (LANES, LANES), 0) == lax.broadcasted_iota(jnp.int32, (LANES, LANES), 1)

    def to_lanes(column):
        return jnp.sum(jnp.where(eye, column, 0.0), axis=0, keepdims=True)

    def to_rows(lanes):
        return jnp.sum(jnp.where(eye, lanes, 0.0), axis=1, keepdims=True)

    col_max = None
    for b in range(IMG // LANES):
        rows = pl.ds(b * LANES, LANES)
        total = None
        for f in range(4):
            term = lax.dot_general(
                img_all[f, rows, :], txt_all[f], (((1,), (1,)), ((), ())), preferred_element_type=F32
            )
            total = term if total is None else total + term
        value = factor * total
        logits[rows, :] = value
        block_max = jnp.max(value, axis=0, keepdims=True)
        col_max = block_max if col_max is None else jnp.maximum(col_max, block_max)

    col_sum = jnp.zeros((1, TXT), F32)
    for b in range(IMG // LANES):
        rows = pl.ds(b * LANES, LANES)
        shifted = jnp.exp(logits[rows, :] - col_max)
        e_col[rows, :] = shifted
        col_sum = col_sum + jnp.sum(shifted, axis=0, keepdims=True)
    lse = col_max + jnp.log(col_sum)
    col_own[pl.ds(0, 1), :] = lse[:, :LANES]
    col_own[pl.ds(1, 1), :] = lse[:, LANES:]
    col_slot = col_recv.at[k]
    col_copies = [
        send(col_own, col_slot, s_col.at[dk], r_col.at[dk], to(in_column(0, dk))) for dk in FAR
    ]
    col_slot[...] = col_own[...]

    for b in range(IMG // LANES):
        rows = pl.ds(b * LANES, LANES)
        value = logits[rows, :]
        largest = jnp.max(value, axis=1, keepdims=True)
        shifted = jnp.exp(value - largest)
        e_row[rows, :] = shifted
        lse = largest + jnp.log(jnp.sum(shifted, axis=1, keepdims=True))
        row_own[pl.ds(b, 1), :] = to_lanes(lse)
        row_max[pl.ds(b, 1), :] = to_lanes(largest)

    row_slot = row_recv.at[q * 16 + (yh * 2 + yl) * NX + x]
    row_copies = []
    for dq in range(2):
        for n, (dx, dy) in enumerate([(0, 0)] + PLANE):
            if dq or n:
                row_copies.append(
                    send(row_own, row_slot, s_row.at[dq, n], r_row.at[dq, n], to(in_plane(dx, dy, dq)))
                )
    row_slot[...] = row_own[...]

    for copy in row_copies:
        copy.wait_recv()
    for copy in col_copies:
        copy.wait_recv()

    def combine(parts):
        largest = jnp.max(parts, axis=0)
        return largest + jnp.log(jnp.sum(jnp.exp(parts - largest[None]), axis=0))

    row_total = combine(row_recv[...])
    row_lse[...] = row_total
    row_mul[...] = 0.5 * jnp.exp(row_max[...] - row_total)
    col_total = combine(col_recv[...])
    col_lse = jnp.concatenate([col_total[0:1], col_total[1:2]], axis=1)
    col_mul = 0.5 * jnp.exp(col_max - col_lse)

    for b in range(IMG // LANES):
        rows = pl.ds(b * LANES, LANES)
        row_factor = to_rows(row_mul[pl.ds(b, 1), :])
        grad[rows, :] = (e_row[rows, :] * row_factor + e_col[rows, :] * col_mul).astype(BF16)
    first = (q * 8 + p) * ROWS + yh * HALF
    diag_rows = pl.ds(pl.multiple_of(first, HALF), HALF)
    row_id = lax.broadcasted_iota(jnp.int32, (HALF, LANES), 0)
    lane_id = lax.broadcasted_iota(jnp.int32, (HALF, LANES), 1)
    pick = lane_id - first % LANES == row_id
    line = pl.ds(first // LANES, 1)
    diag_mul = jnp.sum(jnp.where(pick, row_mul[line, :], 0.0), axis=1, keepdims=True)
    diag_lse = jnp.sum(jnp.where(pick, row_lse[line, :], 0.0), axis=1, keepdims=True)
    row_id = lax.broadcasted_iota(jnp.int32, (HALF, TXT), 0)
    lane_id = lax.broadcasted_iota(jnp.int32, (HALF, TXT), 1)
    unit = lane_id - k * HALF == row_id
    grad[diag_rows, :] = (
        e_row[diag_rows, :] * diag_mul + e_col[diag_rows, :] * col_mul - unit.astype(F32)
    ).astype(BF16)
    loss = jnp.sum(
        jnp.where(unit, 0.5 * (diag_lse + col_lse) - logits[diag_rows, :], 0.0), axis=1, keepdims=True
    )
    loss_all[own_half, :] = jnp.broadcast_to(loss, (HALF, LANES))
    loss_part = loss_all.at[own_half, :]
    loss_copy = send(loss_part, loss_part, s_loss, r_loss, to(in_column(1, 0)))

    ip_copies = []
    for turn in range(2):
        q2 = 1 - q if turn == 0 else q
        rows = pl.ds(pl.multiple_of(q2 * 8 * ROWS, 8 * ROWS), 8 * ROWS)
        for h in range(2):
            i_part[h, rows, :] = jnp.dot(
                grad[rows, :], txt_all[2 * h + c], preferred_element_type=F32
            ).astype(BF16)
        slot = (yh * 2 + yl) * NX + x
        copies = []
        for n, (dx, dy) in enumerate(PLANE):
            place = in_plane(dx, dy)
            block = i_part.at[place[2], image_rows(q2, place[1] * NX + place[0]), :]
            copies.append(send(block, i_recv.at[turn, slot], s_ip.at[turn, n], r_ip.at[turn, n], to(place)))
        i_recv[turn, slot] = i_part[yh, image_rows(q2, p), :]
        ip_copies.append(copies)

    for h in range(2):
        t_part[h] = lax.dot_general(
            grad[...], img_all[2 * h + c], (((0,), (0,)), ((), ())), preferred_element_type=F32
        ).astype(BF16)
    tp_copies = []
    for n, (dh, dk) in enumerate(COLUMN):
        place = in_column(dh, dk)
        rows = pl.ds(pl.multiple_of(((k + dk) % 8) * HALF, HALF), HALF)
        tp_copies.append(
            send(t_part.at[place[2], rows, :], t_recv.at[yh, k], s_tp.at[n], r_tp.at[n], to(place))
        )
    t_recv[yh, k] = t_part[yh, own_cols, :]

    def total_of(ref, count):
        value = ref[0].astype(F32)
        for n in range(1, count):
            value = value + ref[n].astype(F32)
        return value

    for copy in ip_copies[0]:
        copy.wait_recv()
    pair_out[...] = total_of(i_recv.at[0], 16)
    final = send(pair_out, pair_in, s_fin, r_fin, pair)
    for copy in tp_copies:
        copy.wait_recv()
    for h in range(2):
        tg_ref[pl.ds(h * HALF, HALF), :] = total_of(t_recv.at[h], 8)
    loss_copy.wait_recv()
    square = lax.broadcasted_iota(jnp.int32, (ROWS, LANES), 0) == lax.broadcasted_iota(jnp.int32, (ROWS, LANES), 1)
    loss_ref[...] = jnp.sum(jnp.where(square, loss_all[...], 0.0), axis=0, keepdims=True)[:, :ROWS]
    for copy in ip_copies[1]:
        copy.wait_recv()
    own = total_of(i_recv.at[1], 16)
    final.wait_recv()
    ig_ref[...] = own + pair_in[...]
    for copy in started:
        copy.wait_send()


def per_device(image_embeds, text_embeds, logit_scale):
    vmem = pl.BlockSpec(memory_space=pltpu.VMEM)
    hbm = pl.BlockSpec(memory_space=pltpu.HBM)
    dma = pltpu.SemaphoreType.DMA
    column, plane = len(COLUMN), len(PLANE)
    loss, image_grad, text_grad = pl.pallas_call(
        kernel,
        out_shape=(
            jax.ShapeDtypeStruct((1, ROWS), F32),
            jax.ShapeDtypeStruct((ROWS, FEATS), F32),
            jax.ShapeDtypeStruct((ROWS, FEATS), F32),
        ),
        in_specs=[pl.BlockSpec(memory_space=pltpu.SMEM), hbm, hbm],
        out_specs=(vmem, vmem, vmem),
        scratch_shapes=[
            pltpu.VMEM((ROWS, FEATS), BF16),
            pltpu.VMEM((4, IMG, FEATS), BF16),
            pltpu.VMEM((4, TXT, FEATS), BF16),
            pltpu.VMEM((IMG, TXT), F32),
            pltpu.VMEM((IMG, TXT), F32),
            pltpu.VMEM((IMG, TXT), F32),
            pltpu.VMEM((IMG, TXT), BF16),
            pltpu.VMEM((2, IMG, FEATS), BF16),
            pltpu.VMEM((2, TXT, FEATS), BF16),
            pltpu.VMEM((2, 16, ROWS, FEATS), BF16),
            pltpu.VMEM((2, 8, HALF, FEATS), BF16),
            pltpu.VMEM((8, LANES), F32),
            pltpu.VMEM((8, LANES), F32),
            pltpu.VMEM((32, 8, LANES), F32),
            pltpu.VMEM((8, LANES), F32),
            pltpu.VMEM((8, LANES), F32),
            pltpu.VMEM((8, LANES), F32),
            pltpu.VMEM((8, 8, LANES), F32),
            pltpu.VMEM((ROWS, LANES), F32),
            pltpu.VMEM((ROWS, FEATS), F32),
            pltpu.VMEM((ROWS, FEATS), F32),
            dma((2, 8)), dma((2, 8)),
            dma((2, plane)), dma((2, plane)),
            dma, dma,
            dma((2,)), dma((2,)),
            dma((2, 8)), dma((2, 8)),
            dma((16,)), dma((16,)),
            dma((2, 16)), dma((2, 16)),
            dma((8,)), dma((8,)),
            dma, dma,
            dma((column,)), dma((column,)),
            dma((2, plane)), dma((2, plane)),
            dma, dma,
            dma((2,)),
        ],
        compiler_params=pltpu.CompilerParams(
            collective_id=0, has_side_effects=True, vmem_limit_bytes=48 << 20
        ),
    )(logit_scale, image_embeds, text_embeds)
    factor = logit_scale[0]
    return loss.reshape(ROWS), factor * image_grad, factor * text_grad


def solution(mesh):
    return jax.shard_map(
        per_device,
        mesh=mesh,
        in_specs=(P("blk", "feat"), P("blk", "feat"), P()),
        out_specs=(P("blk"), P("blk", "feat"), P("blk", "feat")),
        check_vma=False,
    )
```

```python
import functools

import jax
import jax.numpy as jnp
from jax import lax
from jax.experimental import pallas as pl
from jax.experimental.pallas import tpu as pltpu
from jax.sharding import PartitionSpec as P

MESH = pl.DeviceIdType.MESH
F32 = jnp.float32
BF16 = jnp.bfloat16

NX, NY, NZ = 4, 4, 16
ROWS, FEATS = 64, 256
HALF = ROWS // 2
IMG = 16 * ROWS
TXT = 8 * HALF
LANES = 128

PLANE = sorted([(dx, dy) for dx in range(NX) for dy in range(NY) if dx or dy], key=lambda o: min(o[0], 4 - o[0]) + min(o[1], 4 - o[1]))
FAR = (4, 3, 5, 2, 6, 1, 7)
COLUMN = [(dh, dk) for dk in FAR for dh in range(2)] + [(1, 0)]


def where_am_i():
    blk, feat = lax.axis_index("blk"), lax.axis_index("feat")
    x = blk % NX
    z = (blk // NX) % NZ
    yl = blk // (NX * NZ)
    yh = feat // 2
    return x, yl, yh, z, feat % 2


def device(x, yl, yh, z, c):
    return {"blk": (yl * NZ + z) * NX + x, "feat": yh * 2 + c}


def kernel(
    scale_ref, img_hbm, txt_hbm, loss_ref, ig_ref, tg_ref,
    txt_own,
    img_all, txt_all, logits, e_row, e_col, grad, i_part, t_part, i_recv, t_recv,
    row_own, row_max, row_recv, row_lse, row_mul, col_own, col_recv, loss_all, pair_out, pair_in,
    s_txt, r_txt, s_img, r_img, s_pair, r_pair, s_sib, r_sib, s_sibt, r_sibt, s_sibp, r_sibp,
    s_row, r_row, s_col, r_col, s_loss, r_loss, s_tp, r_tp, s_ip, r_ip, s_fin, r_fin, s_load,
):
    x, yl, yh, z, c = where_am_i()
    q, k = z % 2, z // 2
    feat = yh * 2 + c
    factor = scale_ref[0]

    def in_plane(dx, dy, dq=0):
        x2 = (x + dx) % NX
        y2 = (yh * 2 + yl + dy) % NY
        return x2, y2 % 2, y2 // 2, (z + dq) - 2 * dq * q

    def in_column(dh, dk):
        return x, yl, (yh + dh) % 2, ((k + dk) % 8) * 2 + q

    def to(place):
        return device(*place, c)

    pair = to((x, yl, yh, z + 1 - 2 * q))
    sibling = device(x, yl, yh, z, 1 - c)

    barrier = pltpu.get_barrier_semaphore()
    partners = [to(in_column(0, dk)) for dk in FAR]
    partners += [to(in_plane(dx, dy)) for dx, dy in PLANE]
    partners += [pair, sibling]
    for partner in partners:
        pl.semaphore_signal(barrier, inc=1, device_id=partner, device_id_type=MESH)

    def image_rows(q0, p0):
        return pl.ds(pl.multiple_of((q0 * 8 + p0) * ROWS, ROWS), ROWS)

    p = yl * NX + x
    own_rows = image_rows(q, p)
    own_cols = pl.ds(pl.multiple_of(k * HALF, HALF), HALF)
    own_half = pl.ds(pl.multiple_of(yh * HALF, HALF), HALF)
    own_block = img_all.at[feat, own_rows, :]
    loads = [
        pltpu.make_async_copy(img_hbm, own_block, s_load.at[0]),
        pltpu.make_async_copy(txt_hbm, txt_own, s_load.at[1]),
    ]
    for load in loads:
        load.start()
    col_own[...] = jnp.zeros_like(col_own)
    for load in loads:
        load.wait()
    txt_all[feat, own_cols, :] = txt_own[own_half, :]
    pl.semaphore_wait(barrier, len(partners))

    started = []

    def send(src, dst, s, r, target):
        copy = pltpu.make_async_remote_copy(
            src_ref=src, dst_ref=dst, send_sem=s, recv_sem=r, device_id=target, device_id_type=MESH
        )
        copy.start()
        started.append(copy)
        return copy

    swap = send(own_block, own_block, s_pair, r_pair, pair)
    other_half = pl.ds(pl.multiple_of((1 - yh) * HALF, HALF), HALF)
    own_text = txt_all.at[feat, own_cols, :]
    cross = send(txt_own.at[other_half, :], own_text, s_txt.at[1, 0], r_txt.at[1, 0], to(in_column(1, 0)))
    txt_copies = {
        (0, dk): send(own_text, own_text, s_txt.at[0, dk], r_txt.at[0, dk], to(in_column(0, dk))) for dk in FAR
    }
    direct = [
        send(own_block, own_block, s_img.at[0, n], r_img.at[0, n], to(in_plane(dx, dy)))
        for n, (dx, dy) in enumerate(PLANE)
    ]
    swap.wait_recv()
    pair_block = img_all.at[feat, image_rows(1 - q, p), :]
    passed = [
        send(pair_block, pair_block, s_img.at[1, n], r_img.at[1, n], to(in_plane(dx, dy)))
        for n, (dx, dy) in enumerate(PLANE)
    ]

    cross.wait_recv()
    cross_text = txt_all.at[2 * (1 - yh) + c, own_cols, :]
    for dk in FAR:
        txt_copies[1, dk] = send(cross_text, cross_text, s_txt.at[1, dk], r_txt.at[1, dk], to(in_column(0, dk)))
    shared = []
    for copy in direct:
        copy.wait_recv()
    for h in range(2):
        part = img_all.at[2 * h + c, pl.ds(pl.multiple_of(q * 8 * ROWS, 8 * ROWS), 8 * ROWS), :]
        shared.append(send(part, part, s_sib.at[h], r_sib.at[h], sibling))
    shared.append(send(pair_block, pair_block, s_sibp.at[0], r_sibp.at[0], sibling))
    for dk in (0,) + FAR[::-1]:
        for dh in range(2):
            if dk:
                txt_copies[dh, dk].wait_recv()
            rows = pl.ds(pl.multiple_of(((k - dk + 8) % 8) * HALF, HALF), HALF)
            part = txt_all.at[2 * ((yh + dh) % 2) + c, rows, :]
            shared.append(send(part, part, s_sibt.at[dh, dk], r_sibt.at[dh, dk], sibling))
    for n, (dx, dy) in enumerate(PLANE):
        passed[n].wait_recv()
        x2, yl2, yh2, _ = in_plane(-dx, -dy)
        part = img_all.at[2 * yh2 + c, image_rows(1 - q, yl2 * NX + x2), :]
        shared.append(send(part, part, s_sibp.at[n + 1], r_sibp.at[n + 1], sibling))
    for copy in shared:
        copy.wait_recv()

    eye = lax.broadcasted_iota(jnp.int32, (LANES, LANES), 0) == lax.broadcasted_iota(jnp.int32, (LANES, LANES), 1)

    def to_lanes(column):
        return jnp.sum(jnp.where(eye, column, 0.0), axis=0, keepdims=True)

    def to_rows(lanes):
        return jnp.sum(jnp.where(eye, lanes, 0.0), axis=1, keepdims=True)

    col_max = None
    for b in range(IMG // LANES):
        rows = pl.ds(b * LANES, LANES)
        total = None
        for f in range(4):
            term = lax.dot_general(
                img_all[f, rows, :], txt_all[f], (((1,), (1,)), ((), ())), preferred_element_type=F32
            )
            total = term if total is None else total + term
        value = factor * total
        logits[rows, :] = value
        block_max = jnp.max(value, axis=0, keepdims=True)
        col_max = block_max if col_max is None else jnp.maximum(col_max, block_max)

    col_sum = jnp.zeros((1, TXT), F32)
    for b in range(IMG // LANES):
        rows = pl.ds(b * LANES, LANES)
        shifted = jnp.exp(logits[rows, :] - col_max)
        e_col[rows, :] = shifted
        col_sum = col_sum + jnp.sum(shifted, axis=0, keepdims=True)
    lse = col_max + jnp.log(col_sum)
    col_own[pl.ds(0, 1), :] = lse[:, :LANES]
    col_own[pl.ds(1, 1), :] = lse[:, LANES:]
    col_slot = col_recv.at[k]
    col_copies = [
        send(col_own, col_slot, s_col.at[dk], r_col.at[dk], to(in_column(0, dk))) for dk in FAR
    ]
    col_slot[...] = col_own[...]

    for b in range(IMG // LANES):
        rows = pl.ds(b * LANES, LANES)
        value = logits[rows, :]
        largest = jnp.max(value, axis=1, keepdims=True)
        shifted = jnp.exp(value - largest)
        e_row[rows, :] = shifted
        lse = largest + jnp.log(jnp.sum(shifted, axis=1, keepdims=True))
        row_own[pl.ds(b, 1), :] = to_lanes(lse)
        row_max[pl.ds(b, 1), :] = to_lanes(largest)

    row_slot = row_recv.at[q * 16 + (yh * 2 + yl) * NX + x]
    row_copies = []
    for dq in range(2):
        for n, (dx, dy) in enumerate([(0, 0)] + PLANE):
            if dq or n:
                row_copies.append(
                    send(row_own, row_slot, s_row.at[dq, n], r_row.at[dq, n], to(in_plane(dx, dy, dq)))
                )
    row_slot[...] = row_own[...]

    for copy in row_copies:
        copy.wait_recv()
    for copy in col_copies:
        copy.wait_recv()

    def combine(parts):
        largest = jnp.max(parts, axis=0)
        return largest + jnp.log(jnp.sum(jnp.exp(parts - largest[None]), axis=0))

    row_total = combine(row_recv[...])
    row_lse[...] = row_total
    row_mul[...] = 0.5 * jnp.exp(row_max[...] - row_total)
    col_total = combine(col_recv[...])
    col_lse = jnp.concatenate([col_total[0:1], col_total[1:2]], axis=1)
    col_mul = 0.5 * jnp.exp(col_max - col_lse)

    for b in range(IMG // LANES):
        rows = pl.ds(b * LANES, LANES)
        row_factor = to_rows(row_mul[pl.ds(b, 1), :])
        grad[rows, :] = (e_row[rows, :] * row_factor + e_col[rows, :] * col_mul).astype(BF16)
    first = (q * 8 + p) * ROWS + yh * HALF
    diag_rows = pl.ds(pl.multiple_of(first, HALF), HALF)
    row_id = lax.broadcasted_iota(jnp.int32, (HALF, LANES), 0)
    lane_id = lax.broadcasted_iota(jnp.int32, (HALF, LANES), 1)
    pick = lane_id - first % LANES == row_id
    line = pl.ds(first // LANES, 1)
    diag_mul = jnp.sum(jnp.where(pick, row_mul[line, :], 0.0), axis=1, keepdims=True)
    diag_lse = jnp.sum(jnp.where(pick, row_lse[line, :], 0.0), axis=1, keepdims=True)
    row_id = lax.broadcasted_iota(jnp.int32, (HALF, TXT), 0)
    lane_id = lax.broadcasted_iota(jnp.int32, (HALF, TXT), 1)
    unit = lane_id - k * HALF == row_id
    grad[diag_rows, :] = (
        e_row[diag_rows, :] * diag_mul + e_col[diag_rows, :] * col_mul - unit.astype(F32)
    ).astype(BF16)
    loss = jnp.sum(
        jnp.where(unit, 0.5 * (diag_lse + col_lse) - logits[diag_rows, :], 0.0), axis=1, keepdims=True
    )
    loss_all[own_half, :] = jnp.broadcast_to(loss, (HALF, LANES))
    loss_part = loss_all.at[own_half, :]
    loss_copy = send(loss_part, loss_part, s_loss, r_loss, to(in_column(1, 0)))

    ip_copies = []
    for turn in range(2):
        q2 = 1 - q if turn == 0 else q
        rows = pl.ds(pl.multiple_of(q2 * 8 * ROWS, 8 * ROWS), 8 * ROWS)
        for h in range(2):
            i_part[h, rows, :] = jnp.dot(
                grad[rows, :], txt_all[2 * h + c], preferred_element_type=F32
            ).astype(BF16)
        slot = (yh * 2 + yl) * NX + x
        copies = []
        for n, (dx, dy) in enumerate(PLANE):
            place = in_plane(dx, dy)
            block = i_part.at[place[2], image_rows(q2, place[1] * NX + place[0]), :]
            copies.append(send(block, i_recv.at[turn, slot], s_ip.at[turn, n], r_ip.at[turn, n], to(place)))
        i_recv[turn, slot] = i_part[yh, image_rows(q2, p), :]
        ip_copies.append(copies)

    for h in range(2):
        t_part[h] = lax.dot_general(
            grad[...], img_all[2 * h + c], (((0,), (0,)), ((), ())), preferred_element_type=F32
        ).astype(BF16)
    tp_copies = []
    for n, (dh, dk) in enumerate(COLUMN):
        place = in_column(dh, dk)
        rows = pl.ds(pl.multiple_of(((k + dk) % 8) * HALF, HALF), HALF)
        tp_copies.append(
            send(t_part.at[place[2], rows, :], t_recv.at[yh, k], s_tp.at[n], r_tp.at[n], to(place))
        )
    t_recv[yh, k] = t_part[yh, own_cols, :]

    def total_of(ref, count):
        value = ref[0].astype(F32)
        for n in range(1, count):
            value = value + ref[n].astype(F32)
        return value

    for copy in ip_copies[0]:
        copy.wait_recv()
    pair_out[...] = total_of(i_recv.at[0], 16)
    final = send(pair_out, pair_in, s_fin, r_fin, pair)
    for copy in tp_copies:
        copy.wait_recv()
    for h in range(2):
        tg_ref[pl.ds(h * HALF, HALF), :] = total_of(t_recv.at[h], 8)
    loss_copy.wait_recv()
    square = lax.broadcasted_iota(jnp.int32, (ROWS, LANES), 0) == lax.broadcasted_iota(jnp.int32, (ROWS, LANES), 1)
    loss_ref[...] = jnp.sum(jnp.where(square, loss_all[...], 0.0), axis=0, keepdims=True)[:, :ROWS]
    for copy in ip_copies[1]:
        copy.wait_recv()
    own = total_of(i_recv.at[1], 16)
    final.wait_recv()
    ig_ref[...] = own + pair_in[...]
    for copy in started:
        copy.wait_send()


def per_device(image_embeds, text_embeds, logit_scale):
    vmem = pl.BlockSpec(memory_space=pltpu.VMEM)
    hbm = pl.BlockSpec(memory_space=pltpu.HBM)
    dma = pltpu.SemaphoreType.DMA
    column, plane = len(COLUMN), len(PLANE)
    in_hbm = functools.partial(pltpu.with_memory_space_constraint, memory_space=pltpu.HBM)
    loss, image_grad, text_grad = pl.pallas_call(
        kernel,
        out_shape=(
            jax.ShapeDtypeStruct((1, ROWS), F32),
            jax.ShapeDtypeStruct((ROWS, FEATS), F32),
            jax.ShapeDtypeStruct((ROWS, FEATS), F32),
        ),
        in_specs=[pl.BlockSpec(memory_space=pltpu.SMEM), hbm, hbm],
        out_specs=(vmem, vmem, vmem),
        scratch_shapes=[
            pltpu.VMEM((ROWS, FEATS), BF16),
            pltpu.VMEM((4, IMG, FEATS), BF16),
            pltpu.VMEM((4, TXT, FEATS), BF16),
            pltpu.VMEM((IMG, TXT), F32),
            pltpu.VMEM((IMG, TXT), F32),
            pltpu.VMEM((IMG, TXT), F32),
            pltpu.VMEM((IMG, TXT), BF16),
            pltpu.VMEM((2, IMG, FEATS), BF16),
            pltpu.VMEM((2, TXT, FEATS), BF16),
            pltpu.VMEM((2, 16, ROWS, FEATS), BF16),
            pltpu.VMEM((2, 8, HALF, FEATS), BF16),
            pltpu.VMEM((8, LANES), F32),
            pltpu.VMEM((8, LANES), F32),
            pltpu.VMEM((32, 8, LANES), F32),
            pltpu.VMEM((8, LANES), F32),
            pltpu.VMEM((8, LANES), F32),
            pltpu.VMEM((8, LANES), F32),
            pltpu.VMEM((8, 8, LANES), F32),
            pltpu.VMEM((ROWS, LANES), F32),
            pltpu.VMEM((ROWS, FEATS), F32),
            pltpu.VMEM((ROWS, FEATS), F32),
            dma((2, 8)), dma((2, 8)),
            dma((2, plane)), dma((2, plane)),
            dma, dma,
            dma((2,)), dma((2,)),
            dma((2, 8)), dma((2, 8)),
            dma((16,)), dma((16,)),
            dma((2, 16)), dma((2, 16)),
            dma((8,)), dma((8,)),
            dma, dma,
            dma((column,)), dma((column,)),
            dma((2, plane)), dma((2, plane)),
            dma, dma,
            dma((2,)),
        ],
        compiler_params=pltpu.CompilerParams(
            collective_id=0, has_side_effects=True, vmem_limit_bytes=48 << 20
        ),
    )(logit_scale, in_hbm(image_embeds), in_hbm(text_embeds))
    factor = logit_scale[0]
    return loss.reshape(ROWS), factor * image_grad, factor * text_grad


def solution(mesh):
    return jax.shard_map(
        per_device,
        mesh=mesh,
        in_specs=(P("blk", "feat"), P("blk", "feat"), P()),
        out_specs=(P("blk"), P("blk", "feat"), P("blk", "feat")),
        check_vma=False,
    )
```

```python
import functools

import jax
import jax.numpy as jnp
from jax import lax
from jax.experimental import pallas as pl
from jax.experimental.pallas import tpu as pltpu
from jax.sharding import PartitionSpec as P

MESH = pl.DeviceIdType.MESH
F32 = jnp.float32
BF16 = jnp.bfloat16

NX, NY, NZ = 4, 4, 16
ROWS, FEATS = 64, 256
HALF = ROWS // 2
IMG = 16 * ROWS
TXT = 8 * HALF
LANES = 128

PLANE = sorted([(dx, dy) for dx in range(NX) for dy in range(NY) if dx or dy], key=lambda o: min(o[0], 4 - o[0]) + min(o[1], 4 - o[1]))
FAR = (4, 3, 5, 2, 6, 1, 7)
COLUMN = [(dh, dk) for dk in FAR for dh in range(2)] + [(1, 0)]


def where_am_i():
    blk, feat = lax.axis_index("blk"), lax.axis_index("feat")
    x = blk % NX
    z = (blk // NX) % NZ
    yl = blk // (NX * NZ)
    yh = feat // 2
    return x, yl, yh, z, feat % 2


def device(x, yl, yh, z, c):
    return {"blk": (yl * NZ + z) * NX + x, "feat": yh * 2 + c}


def kernel(
    scale_ref, img_hbm, txt_hbm, loss_ref, ig_ref, tg_ref,
    txt_own,
    img_all, txt_all, logits, e_row, e_col, grad, i_part, t_part, i_recv, t_recv,
    row_own, row_max, row_recv, row_lse, row_mul, col_own, col_recv, loss_all, pair_out, pair_in,
    s_txt, r_txt, s_img, r_img, s_pair, r_pair, s_sib, r_sib, s_sibt, r_sibt, s_sibp, r_sibp,
    s_row, r_row, s_col, r_col, s_loss, r_loss, s_tp, r_tp, s_ip, r_ip, s_fin, r_fin, s_load,
):
    x, yl, yh, z, c = where_am_i()
    q, k = z % 2, z // 2
    feat = yh * 2 + c
    factor = scale_ref[0]

    def in_plane(dx, dy, dq=0):
        x2 = (x + dx) % NX
        y2 = (yh * 2 + yl + dy) % NY
        return x2, y2 % 2, y2 // 2, (z + dq) - 2 * dq * q

    def in_column(dh, dk):
        return x, yl, (yh + dh) % 2, ((k + dk) % 8) * 2 + q

    def to(place):
        return device(*place, c)

    pair = to((x, yl, yh, z + 1 - 2 * q))
    sibling = device(x, yl, yh, z, 1 - c)

    barrier = pltpu.get_barrier_semaphore()
    partners = [to(in_column(0, dk)) for dk in FAR]
    partners += [to(in_plane(dx, dy)) for dx, dy in PLANE]
    partners += [pair, sibling]
    for partner in partners:
        pl.semaphore_signal(barrier, inc=1, device_id=partner, device_id_type=MESH)

    def image_rows(q0, p0):
        return pl.ds(pl.multiple_of((q0 * 8 + p0) * ROWS, ROWS), ROWS)

    p = yl * NX + x
    own_rows = image_rows(q, p)
    own_cols = pl.ds(pl.multiple_of(k * HALF, HALF), HALF)
    own_half = pl.ds(pl.multiple_of(yh * HALF, HALF), HALF)
    own_block = img_all.at[feat, own_rows, :]
    loads = [
        pltpu.make_async_copy(img_hbm, own_block, s_load.at[0]),
        pltpu.make_async_copy(txt_hbm, txt_own, s_load.at[1]),
    ]
    for load in loads:
        load.start()
    col_own[...] = jnp.zeros_like(col_own)
    for load in loads:
        load.wait()
    txt_all[feat, own_cols, :] = txt_own[own_half, :]
    pl.semaphore_wait(barrier, len(partners))

    started = []

    def send(src, dst, s, r, target):
        copy = pltpu.make_async_remote_copy(
            src_ref=src, dst_ref=dst, send_sem=s, recv_sem=r, device_id=target, device_id_type=MESH
        )
        copy.start()
        started.append(copy)
        return copy

    swap = send(own_block, own_block, s_pair, r_pair, pair)
    other_half = pl.ds(pl.multiple_of((1 - yh) * HALF, HALF), HALF)
    own_text = txt_all.at[feat, own_cols, :]
    cross = send(txt_own.at[other_half, :], own_text, s_txt.at[1, 0], r_txt.at[1, 0], to(in_column(1, 0)))
    txt_copies = {
        (0, dk): send(own_text, own_text, s_txt.at[0, dk], r_txt.at[0, dk], to(in_column(0, dk))) for dk in FAR
    }
    direct = [
        send(own_block, own_block, s_img.at[0, n], r_img.at[0, n], to(in_plane(dx, dy)))
        for n, (dx, dy) in enumerate(PLANE)
    ]
    swap.wait_recv()
    pair_block = img_all.at[feat, image_rows(1 - q, p), :]
    passed = [
        send(pair_block, pair_block, s_img.at[1, n], r_img.at[1, n], to(in_plane(dx, dy)))
        for n, (dx, dy) in enumerate(PLANE)
    ]

    cross.wait_recv()
    cross_text = txt_all.at[2 * (1 - yh) + c, own_cols, :]
    for dk in FAR:
        txt_copies[1, dk] = send(cross_text, cross_text, s_txt.at[1, dk], r_txt.at[1, dk], to(in_column(0, dk)))
    shared = []
    for copy in direct:
        copy.wait_recv()
    for h in range(2):
        part = img_all.at[2 * h + c, pl.ds(pl.multiple_of(q * 8 * ROWS, 8 * ROWS), 8 * ROWS), :]
        shared.append(send(part, part, s_sib.at[h], r_sib.at[h], sibling))
    shared.append(send(pair_block, pair_block, s_sibp.at[0], r_sibp.at[0], sibling))
    for dk in (0,) + FAR[::-1]:
        for dh in range(2):
            if dk:
                txt_copies[dh, dk].wait_recv()
            rows = pl.ds(pl.multiple_of(((k - dk + 8) % 8) * HALF, HALF), HALF)
            part = txt_all.at[2 * ((yh + dh) % 2) + c, rows, :]
            shared.append(send(part, part, s_sibt.at[dh, dk], r_sibt.at[dh, dk], sibling))
    for n, (dx, dy) in enumerate(PLANE):
        passed[n].wait_recv()
        x2, yl2, yh2, _ = in_plane(-dx, -dy)
        part = img_all.at[2 * yh2 + c, image_rows(1 - q, yl2 * NX + x2), :]
        shared.append(send(part, part, s_sibp.at[n + 1], r_sibp.at[n + 1], sibling))
    for copy in shared:
        copy.wait_recv()

    eye = lax.broadcasted_iota(jnp.int32, (LANES, LANES), 0) == lax.broadcasted_iota(jnp.int32, (LANES, LANES), 1)

    def to_lanes(column):
        return jnp.sum(jnp.where(eye, column, 0.0), axis=0, keepdims=True)

    def to_rows(lanes):
        return jnp.sum(jnp.where(eye, lanes, 0.0), axis=1, keepdims=True)

    col_max = None
    for b in range(IMG // LANES):
        rows = pl.ds(b * LANES, LANES)
        total = None
        for f in range(4):
            term = lax.dot_general(
                img_all[f, rows, :], txt_all[f], (((1,), (1,)), ((), ())), preferred_element_type=F32
            )
            total = term if total is None else total + term
        value = factor * total
        logits[rows, :] = value
        block_max = jnp.max(value, axis=0, keepdims=True)
        col_max = block_max if col_max is None else jnp.maximum(col_max, block_max)

    col_sum = jnp.zeros((1, TXT), F32)
    for b in range(IMG // LANES):
        rows = pl.ds(b * LANES, LANES)
        shifted = jnp.exp(logits[rows, :] - col_max)
        e_col[rows, :] = shifted
        col_sum = col_sum + jnp.sum(shifted, axis=0, keepdims=True)
    lse = col_max + jnp.log(col_sum)
    col_own[pl.ds(0, 1), :] = lse[:, :LANES]
    col_own[pl.ds(1, 1), :] = lse[:, LANES:]
    col_slot = col_recv.at[k]
    col_copies = [
        send(col_own, col_slot, s_col.at[dk], r_col.at[dk], to(in_column(0, dk))) for dk in FAR
    ]
    col_slot[...] = col_own[...]

    for b in range(IMG // LANES):
        rows = pl.ds(b * LANES, LANES)
        value = logits[rows, :]
        largest = jnp.max(value, axis=1, keepdims=True)
        shifted = jnp.exp(value - largest)
        e_row[rows, :] = shifted
        lse = largest + jnp.log(jnp.sum(shifted, axis=1, keepdims=True))
        row_own[pl.ds(b, 1), :] = to_lanes(lse)
        row_max[pl.ds(b, 1), :] = to_lanes(largest)

    row_slot = row_recv.at[q * 16 + (yh * 2 + yl) * NX + x]
    row_copies = []
    for dq in range(2):
        for n, (dx, dy) in enumerate([(0, 0)] + PLANE):
            if dq or n:
                row_copies.append(
                    send(row_own, row_slot, s_row.at[dq, n], r_row.at[dq, n], to(in_plane(dx, dy, dq)))
                )
    row_slot[...] = row_own[...]

    for copy in row_copies:
        copy.wait_recv()
    for copy in col_copies:
        copy.wait_recv()

    def combine(parts):
        largest = jnp.max(parts, axis=0)
        return largest + jnp.log(jnp.sum(jnp.exp(parts - largest[None]), axis=0))

    row_total = combine(row_recv[...])
    row_lse[...] = row_total
    row_mul[...] = 0.5 * jnp.exp(row_max[...] - row_total)
    col_total = combine(col_recv[...])
    col_lse = jnp.concatenate([col_total[0:1], col_total[1:2]], axis=1)
    col_mul = 0.5 * jnp.exp(col_max - col_lse)

    def gradient(q2):
        for b in range(4):
            rows = pl.ds(pl.multiple_of(q2 * (8 * ROWS) + b * LANES, LANES), LANES)
            row_factor = to_rows(row_mul[pl.ds(q2 * 4 + b, 1), :])
            grad[rows, :] = (e_row[rows, :] * row_factor + e_col[rows, :] * col_mul).astype(BF16)

    ip_copies = []
    def image_turn(turn):
        q2 = 1 - q if turn == 0 else q
        rows = pl.ds(pl.multiple_of(q2 * 8 * ROWS, 8 * ROWS), 8 * ROWS)
        for h in range(2):
            i_part[h, rows, :] = jnp.dot(
                grad[rows, :], txt_all[2 * h + c], preferred_element_type=F32
            ).astype(BF16)
        slot = (yh * 2 + yl) * NX + x
        copies = []
        for n, (dx, dy) in enumerate(PLANE):
            place = in_plane(dx, dy)
            block = i_part.at[place[2], image_rows(q2, place[1] * NX + place[0]), :]
            copies.append(send(block, i_recv.at[turn, slot], s_ip.at[turn, n], r_ip.at[turn, n], to(place)))
        i_recv[turn, slot] = i_part[yh, image_rows(q2, p), :]
        ip_copies.append(copies)

    gradient(1 - q)
    image_turn(0)
    gradient(q)
    first = (q * 8 + p) * ROWS + yh * HALF
    diag_rows = pl.ds(pl.multiple_of(first, HALF), HALF)
    row_id = lax.broadcasted_iota(jnp.int32, (HALF, LANES), 0)
    lane_id = lax.broadcasted_iota(jnp.int32, (HALF, LANES), 1)
    pick = lane_id - first % LANES == row_id
    line = pl.ds(first // LANES, 1)
    diag_mul = jnp.sum(jnp.where(pick, row_mul[line, :], 0.0), axis=1, keepdims=True)
    diag_lse = jnp.sum(jnp.where(pick, row_lse[line, :], 0.0), axis=1, keepdims=True)
    row_id = lax.broadcasted_iota(jnp.int32, (HALF, TXT), 0)
    lane_id = lax.broadcasted_iota(jnp.int32, (HALF, TXT), 1)
    unit = lane_id - k * HALF == row_id
    grad[diag_rows, :] = (
        e_row[diag_rows, :] * diag_mul + e_col[diag_rows, :] * col_mul - unit.astype(F32)
    ).astype(BF16)
    image_turn(1)
    loss = jnp.sum(
        jnp.where(unit, 0.5 * (diag_lse + col_lse) - logits[diag_rows, :], 0.0), axis=1, keepdims=True
    )
    loss_all[own_half, :] = jnp.broadcast_to(loss, (HALF, LANES))
    loss_part = loss_all.at[own_half, :]
    loss_copy = send(loss_part, loss_part, s_loss, r_loss, to(in_column(1, 0)))

    for h in range(2):
        t_part[h] = lax.dot_general(
            grad[...], img_all[2 * h + c], (((0,), (0,)), ((), ())), preferred_element_type=F32
        ).astype(BF16)
    tp_copies = []
    for n, (dh, dk) in enumerate(COLUMN):
        place = in_column(dh, dk)
        rows = pl.ds(pl.multiple_of(((k + dk) % 8) * HALF, HALF), HALF)
        tp_copies.append(
            send(t_part.at[place[2], rows, :], t_recv.at[yh, k], s_tp.at[n], r_tp.at[n], to(place))
        )
    t_recv[yh, k] = t_part[yh, own_cols, :]

    def total_of(ref, count):
        value = ref[0].astype(F32)
        for n in range(1, count):
            value = value + ref[n].astype(F32)
        return value

    for copy in ip_copies[0]:
        copy.wait_recv()
    pair_out[...] = total_of(i_recv.at[0], 16)
    final = send(pair_out, pair_in, s_fin, r_fin, pair)
    for copy in tp_copies:
        copy.wait_recv()
    for h in range(2):
        tg_ref[pl.ds(h * HALF, HALF), :] = total_of(t_recv.at[h], 8)
    loss_copy.wait_recv()
    square = lax.broadcasted_iota(jnp.int32, (ROWS, LANES), 0) == lax.broadcasted_iota(jnp.int32, (ROWS, LANES), 1)
    loss_ref[...] = jnp.sum(jnp.where(square, loss_all[...], 0.0), axis=0, keepdims=True)[:, :ROWS]
    for copy in ip_copies[1]:
        copy.wait_recv()
    own = total_of(i_recv.at[1], 16)
    final.wait_recv()
    ig_ref[...] = own + pair_in[...]
    for copy in started:
        copy.wait_send()


def per_device(image_embeds, text_embeds, logit_scale):
    vmem = pl.BlockSpec(memory_space=pltpu.VMEM)
    hbm = pl.BlockSpec(memory_space=pltpu.HBM)
    dma = pltpu.SemaphoreType.DMA
    column, plane = len(COLUMN), len(PLANE)
    in_hbm = functools.partial(pltpu.with_memory_space_constraint, memory_space=pltpu.HBM)
    loss, image_grad, text_grad = pl.pallas_call(
        kernel,
        out_shape=(
            jax.ShapeDtypeStruct((1, ROWS), F32),
            jax.ShapeDtypeStruct((ROWS, FEATS), F32),
            jax.ShapeDtypeStruct((ROWS, FEATS), F32),
        ),
        in_specs=[pl.BlockSpec(memory_space=pltpu.SMEM), hbm, hbm],
        out_specs=(vmem, vmem, vmem),
        scratch_shapes=[
            pltpu.VMEM((ROWS, FEATS), BF16),
            pltpu.VMEM((4, IMG, FEATS), BF16),
            pltpu.VMEM((4, TXT, FEATS), BF16),
            pltpu.VMEM((IMG, TXT), F32),
            pltpu.VMEM((IMG, TXT), F32),
            pltpu.VMEM((IMG, TXT), F32),
            pltpu.VMEM((IMG, TXT), BF16),
            pltpu.VMEM((2, IMG, FEATS), BF16),
            pltpu.VMEM((2, TXT, FEATS), BF16),
            pltpu.VMEM((2, 16, ROWS, FEATS), BF16),
            pltpu.VMEM((2, 8, HALF, FEATS), BF16),
            pltpu.VMEM((8, LANES), F32),
            pltpu.VMEM((8, LANES), F32),
            pltpu.VMEM((32, 8, LANES), F32),
            pltpu.VMEM((8, LANES), F32),
            pltpu.VMEM((8, LANES), F32),
            pltpu.VMEM((8, LANES), F32),
            pltpu.VMEM((8, 8, LANES), F32),
            pltpu.VMEM((ROWS, LANES), F32),
            pltpu.VMEM((ROWS, FEATS), F32),
            pltpu.VMEM((ROWS, FEATS), F32),
            dma((2, 8)), dma((2, 8)),
            dma((2, plane)), dma((2, plane)),
            dma, dma,
            dma((2,)), dma((2,)),
            dma((2, 8)), dma((2, 8)),
            dma((16,)), dma((16,)),
            dma((2, 16)), dma((2, 16)),
            dma((8,)), dma((8,)),
            dma, dma,
            dma((column,)), dma((column,)),
            dma((2, plane)), dma((2, plane)),
            dma, dma,
            dma((2,)),
        ],
        compiler_params=pltpu.CompilerParams(
            collective_id=0, has_side_effects=True, vmem_limit_bytes=48 << 20
        ),
    )(logit_scale, in_hbm(image_embeds), in_hbm(text_embeds))
    factor = logit_scale[0]
    return loss.reshape(ROWS), factor * image_grad, factor * text_grad


def solution(mesh):
    return jax.shard_map(
        per_device,
        mesh=mesh,
        in_specs=(P("blk", "feat"), P("blk", "feat"), P()),
        out_specs=(P("blk"), P("blk", "feat"), P("blk", "feat")),
        check_vma=False,
    )
```
